32 devices in a mesh: groups: 2 (over x), dev: 16 (over z, y, core).
Axes of the slice: x: 2, y: 2, z: 4, core: 2. Of those that a mesh axis runs over, the one named last changes fastest.
Arguments:
- hidden: bfloat16 [64, 384, 4608], P(('groups', 'dev')), parts along dimension 0, may hold values from -6 to 6
- norm_gain: bfloat16 [4608], replicated, may hold values from 0.099609375 to 1.8984375
- w_key: bfloat16 [4608, 1024], P('dev'), may hold values from -0.09375 to 0.09375
- w_value: bfloat16 [4608, 1024], P('dev'), may hold values from -0.09375 to 0.09375
- queries: bfloat16 [32, 4, 2048], P(('groups', 'dev')), parts along dimension 0, may hold values from -174 to 174
- new_keys: bfloat16 [32, 4, 1024], P(('groups', 'dev')), parts along dimension 0, may hold values from -6 to 6
- new_values: bfloat16 [32, 4, 1024], P(('groups', 'dev')), parts along dimension 0, may hold values from -6 to 6
- passage_owner: int32 [64], P('groups'), parts along dimension 0, may hold values from 0 to 15, as said below
Outputs:
- attended: bfloat16 [32, 4, 2048], P(('groups', 'dev')), parts along dimension 0
The draws below stay inside these ranges and needn't reach their ends.
There are 2 independent parts, one for each index of `groups`. The reference program is written for one: setup_inputs(seed, part) draws one part's arguments, and reference() takes and returns one part's arrays. A program takes and returns all parts, laid end to end along the dimension named above; an argument that names none is the same for every part. Nothing has to cross between parts.
Inputs may be any that keep to these rules, and one draw needn't show every extreme that they name: Passage p lies on device p // 2 and belongs to the request owned by device passage_owner[p], which lies at most 1 positions from that device along dev, counted cyclically; in each direction some passage lies exactly 1 away.
All inputs are finite; a program needn't handle non-finite values.
Results may differ from the reference program's by a relative error of at most 0.0049.
Values may be sent and summed in bfloat16 or wider, within the bound.
A program may use at most 128 MiB of HBM per device.

```python
from functools import partial
import jax
import jax.numpy as jnp
from jax import lax

D = 4608
HEAD_DIM = 128
KV_HEADS = 8
Q_HEADS = 16
PASS_LEN = 384
PASS_DEV = 2
STEPS = 4
REACH = 1
PASSAGES = 32
REQUESTS = 16


def shared_fresh(key):
    shape_fresh = (REQUESTS, STEPS, KV_HEADS, HEAD_DIM)
    normal_part = jnp.clip(jax.random.normal(key, shape_fresh, jnp.float32), -6.0, 6.0)
    return normal_part


def draw_new_keys(key, part):
    fresh_base = shared_fresh(key)
    return fresh_base.reshape(REQUESTS, STEPS, KV_HEADS * HEAD_DIM).astype(jnp.bfloat16)


def draw_queries(key, part):
    fresh_base = shared_fresh(key)
    key = jax.random.fold_in(key, 13)
    mask_key, target_key, normal_key = jax.random.split(key, 3)
    per_group = Q_HEADS // KV_HEADS
    shape_query = (REQUESTS, STEPS, KV_HEADS, per_group, HEAD_DIM)
    normal_noise = jnp.clip(jax.random.normal(normal_key, shape_query, jnp.float32), -6.0, 6.0)
    query_noise = normal_noise
    chosen = jax.random.bernoulli(mask_key, 0.25, (REQUESTS, KV_HEADS, per_group))
    chosen = chosen.at[0, 0, 0].set(True)
    target = jnp.exp(jax.random.uniform(target_key, (REQUESTS, KV_HEADS, per_group), jnp.float32, jnp.log(50.0), jnp.log(150.0)))
    strength = target * 12.0 / HEAD_DIM
    pair_sum = fresh_base[:, 0] + fresh_base[:, 1]
    aligned = strength[..., None] * pair_sum[:, :, None, :]
    last_step = jnp.where(chosen[..., None], aligned, query_noise[:, STEPS - 1])
    full_query = query_noise.at[:, STEPS - 1].set(last_step)
    return full_query.reshape(REQUESTS, STEPS, Q_HEADS * HEAD_DIM).astype(jnp.bfloat16)


def draw_passage_owner(key, part):
    key = jax.random.fold_in(key, 7)
    offsets = jax.random.randint(key, (PASSAGES,), -REACH, REACH + 1)
    offsets = offsets.at[0].set(REACH).at[1].set(-REACH).at[PASS_DEV].set(-REACH)
    home_device = jnp.arange(PASSAGES, dtype=jnp.int32) // PASS_DEV
    return ((home_device + offsets) % REQUESTS).astype(jnp.int32)


def level_of(own_key, extent, cuts, least, largest):
    def one(axis_at, blocks):
        draws = jax.random.uniform(jax.random.fold_in(jax.random.fold_in(own_key, 6), axis_at), (blocks,), jnp.float32, least / len(cuts), largest / len(cuts))
        return jnp.repeat(jnp.exp(draws), extent[axis_at] // blocks).reshape((-1,) + (1,) * (len(extent) - axis_at - 1))

    factor_of = one(*cuts[0])
    for cut in cuts[1:]:
        factor_of = factor_of * one(*cut)
    return factor_of


def normal_values(own_key, dims, width, limit, cuts=(), kind=jnp.bfloat16):
    level = level_of(own_key, dims, cuts, -0.22, 0.18) if cuts else 1.0
    array = jax.random.normal(own_key, dims, jnp.float32) * width * level
    return jnp.minimum(jnp.maximum(array, -limit), limit).astype(kind)


def setup_inputs(seed: int = 0, part: int = 0) -> dict:
    streams_of = jax.random.split(jax.random.key(seed), 9)
    part_splits = jax.random.split(jax.random.fold_in(streams_of[8], part), 9)
    return {
        "hidden": normal_values(part_splits[0], (PASSAGES, PASS_LEN, D), 1.0, 6.0, ((0, 16),)),
        "norm_gain": jnp.clip(1.0 + 0.18 * jax.random.normal(streams_of[1], (D,), jnp.float32), 0.099609375, 1.8984375).astype(jnp.bfloat16),
        "w_key": normal_values(streams_of[2], (D, KV_HEADS * HEAD_DIM), D ** -0.5, 0.09375, ((0, 16),)),
        "w_value": normal_values(streams_of[3], (D, KV_HEADS * HEAD_DIM), D ** -0.5, 0.09375, ((0, 16),)),
        "queries": draw_queries(jax.random.fold_in(jax.random.fold_in(streams_of[8], part), 71), part),
        "new_keys": draw_new_keys(jax.random.fold_in(jax.random.fold_in(streams_of[8], part), 71), part),
        "new_values": normal_values(part_splits[6], (REQUESTS, STEPS, KV_HEADS * HEAD_DIM), 1.0, 6.0, ((0, 16),)),
        "passage_owner": draw_passage_owner(jax.random.fold_in(jax.random.fold_in(streams_of[8], part), 71), part),
    }


CAP_LIMIT = 50.0
QUERY_SCALE = 1.0 / 12.0
EPSILON = 1e-06

def rotate_keys(raw_keys, head_count, head_width):
    length = raw_keys.shape[0]
    half_width = head_width // 2
    blocked = raw_keys.reshape(length, head_count, head_width)
    position = jnp.arange(length, dtype=jnp.float32)
    inverse = 10000.0 ** (-(jnp.arange(half_width, dtype=jnp.float32) * 2.0) / head_width)
    angles = position[:, None] * inverse[None, :]
    cosine = jnp.cos(angles)[:, None, :]
    sine_part = jnp.sin(angles)[:, None, :]
    lower_half = blocked[:, :, :half_width]
    upper_half = blocked[:, :, half_width:]
    turned = jnp.concatenate([lower_half * cosine - upper_half * sine_part, upper_half * cosine + lower_half * sine_part], axis=-1)
    return turned.reshape(length, head_count * head_width)

def encode_passage(passage_rows, norm_gain, w_key, w_value):
    values32 = passage_rows.astype(jnp.float32)
    mean_square = lax.optimization_barrier(jnp.mean(values32 * values32, axis=-1, keepdims=True))
    normed = (values32 * lax.rsqrt(mean_square + EPSILON) * norm_gain.astype(jnp.float32)).astype(jnp.bfloat16)
    raw_keys = jnp.dot(normed, w_key, preferred_element_type=jnp.float32)
    cache_keys = rotate_keys(raw_keys, KV_HEADS, HEAD_DIM).astype(jnp.bfloat16)
    cache_values = jnp.dot(normed, w_value, preferred_element_type=jnp.float32).astype(jnp.bfloat16)
    return (cache_keys, cache_values)

def capped_weights(grouped, key_rows):
    scores = jnp.einsum('sghd,kgd->sghk', grouped, key_rows)
    return jnp.exp(CAP_LIMIT * jnp.tanh(scores * QUERY_SCALE / CAP_LIMIT))

def reference(hidden, norm_gain, w_key, w_value, queries, new_keys, new_values, passage_owner):
    encoder = partial(encode_passage, norm_gain=norm_gain, w_key=w_key, w_value=w_value)
    cache_keys, cache_values = lax.map(encoder, hidden)
    all_keys = cache_keys.reshape(PASSAGES * PASS_LEN, KV_HEADS, HEAD_DIM).astype(jnp.float32)
    all_values = cache_values.reshape(PASSAGES * PASS_LEN, KV_HEADS, HEAD_DIM).astype(jnp.float32)
    key_owner = jnp.repeat(passage_owner.astype(jnp.int32), PASS_LEN)
    causal = jnp.arange(STEPS)[:, None] >= jnp.arange(STEPS)[None, :]

    def one_request(request_item):
        request, query_rows, fresh_keys, fresh_values = request_item
        grouped = query_rows.astype(jnp.float32).reshape(STEPS, KV_HEADS, Q_HEADS // KV_HEADS, HEAD_DIM)
        weights = capped_weights(grouped, all_keys)
        weights = jnp.where((key_owner == request)[None, None, None, :], weights, jnp.float32(0.0))
        fresh_rows = fresh_keys.astype(jnp.float32).reshape(STEPS, KV_HEADS, HEAD_DIM)
        fresh_weights = capped_weights(grouped, fresh_rows)
        fresh_weights = jnp.where(causal[:, None, None, :], fresh_weights, jnp.float32(0.0))
        denominator = lax.optimization_barrier(jnp.sum(weights, axis=-1)) + lax.optimization_barrier(jnp.sum(fresh_weights, axis=-1))
        rounded = lax.optimization_barrier(weights.astype(jnp.bfloat16)).astype(jnp.float32)
        fresh_rounded = lax.optimization_barrier(fresh_weights.astype(jnp.bfloat16)).astype(jnp.float32)
        fresh_vals = fresh_values.astype(jnp.float32).reshape(STEPS, KV_HEADS, HEAD_DIM)
        numerator = jnp.einsum('sghk,kgd->sghd', rounded, all_values)
        numerator = numerator + jnp.einsum('sghk,kgd->sghd', fresh_rounded, fresh_vals)
        result = numerator / denominator[..., None]
        return result.reshape(STEPS, Q_HEADS * HEAD_DIM).astype(jnp.bfloat16)
    request_ids = jnp.arange(REQUESTS, dtype=jnp.int32)
    return lax.map(one_request, (request_ids, queries, new_keys, new_values))
```

```python
import functools

import jax
import jax.numpy as jnp
import numpy as np
from jax import lax
from jax.experimental import pallas as pl
from jax.experimental.pallas import tpu as pltpu
from jax.sharding import PartitionSpec as P

HEAD_DIM = 128
KV_HEADS = 8
Q_HEADS = 16
STEPS = 4
ROWS = STEPS * Q_HEADS

CAP_LIMIT = 50.0
QUERY_SCALE = 1.0 / 12.0
EPSILON = 1e-06

SIDE = 256
MIDDLE = 512
MESH = pl.DeviceIdType.MESH


def rotation_tables(length):
    half = HEAD_DIM // 2
    inverse = 10000.0 ** (-(np.arange(half, dtype=np.float64) * 2.0) / HEAD_DIM)
    angles = np.arange(length, dtype=np.float64)[:, None] * inverse[None, :]
    cosine, sine = np.cos(angles), np.sin(angles)
    return (
        np.concatenate([cosine, cosine], axis=1).astype(np.float32),
        np.concatenate([-sine, sine], axis=1).astype(np.float32),
    )


def softcap_exp(scores):
    return jnp.exp(CAP_LIMIT * jnp.tanh(scores * (QUERY_SCALE / CAP_LIMIT)))


def dot_t(a, b):
    return lax.dot_general(a, b, (((1,), (1,)), ((), ())), preferred_element_type=jnp.float32)


def kernel(
    snake, hidden, gain, w_key, w_value, queries, new_keys, new_values, cosines, sines, owner,
    out,
    raw, normed, weights, sums, query_rows, got_queries, fresh_rows, scores, dens, nums, sent, got, out32,
    hidden_sem, own_sem, a_send, a_recv, b_send, b_recv, x_send, x_recv,
    so_send, so_recv, sa_send, sa_recv, sb_send, sb_recv, sx_send, sx_recv,
    q_send, q_recv, r_send, r_recv,
):
    devices = lax.axis_size("dev")
    chips = devices // 2
    group = lax.axis_index("groups")
    me = lax.axis_index("dev")
    chip, core = me // 2, me % 2
    odd = group % 2
    partner = group + 1 - 2 * odd
    passages, length, width = hidden.shape
    depth = width // devices

    def chip_at(place):
        place = lax.rem(place + 2 * chips, chips)
        if not snake:
            return place
        return jnp.where(place < chips // 2, 2 * place, 2 * (chips - 1 - place) + 1)

    if snake:
        place = jnp.where(chip % 2 == 0, chip // 2, chips - 1 - chip // 2)
    else:
        place = chip

    def device_at(position, which):
        return chip_at(position) * 2 + which

    ahead, behind = device_at(place + 1, core), device_at(place - 1, core)
    sibling = chip * 2 + 1 - core
    right, left = lax.rem(me + 1, devices), lax.rem(me + devices - 1, devices)

    barrier = pltpu.get_barrier_semaphore()
    friends = [(group, ahead), (group, behind), (group, sibling), (partner, me), (group, right), (group, left)]
    for friend in friends:
        pl.semaphore_signal(barrier, inc=1, device_id=friend, device_id_type=MESH)

    loads = [
        pltpu.make_async_copy(hidden.at[p], raw.at[p], hidden_sem.at[p]) for p in range(passages)
    ]
    for load in loads:
        load.start()
    sources = (w_key, w_value)
    own_loads = [
        pltpu.make_async_copy(sources[m], weights.at[m, me], own_sem.at[m]) for m in range(2)
    ]
    for load in own_loads:
        load.start()

    side = pl.ds(pl.multiple_of(odd * (SIDE + MIDDLE), 128), SIDE)
    other_side = pl.ds(pl.multiple_of((1 - odd) * (SIDE + MIDDLE), 128), SIDE)
    middle = pl.ds(SIDE, MIDDLE)

    def remote(src, dst, send, recv, target):
        return pltpu.make_async_remote_copy(
            src_ref=src, dst_ref=dst, send_sem=send, recv_sem=recv, device_id=target, device_id_type=MESH
        )

    sign = (1, -1)
    a_target = ((group, ahead), (group, behind))
    b_target = ((group, behind), (group, ahead))

    def block(m, e, columns):
        return weights.at[m, e, :, columns]

    def a_from(m, s, which):
        return device_at(place - sign[m] * s, which)

    def b_from(m, s, which):
        return device_at(place + sign[m] * s, which)

    def send_a(m, s):
        e = a_from(m, s - 1, core)
        ref = block(m, e, side)
        return remote(ref, ref, a_send.at[m, s], a_recv.at[m, s], a_target[m])

    def send_b(m, s):
        e = b_from(m, s - 1, core)
        ref = block(m, e, middle)
        return remote(ref, ref, b_send.at[m, s], b_recv.at[m, s], b_target[m])

    def recv_a(m, s):
        ref = block(m, a_from(m, s, core), side)
        return remote(ref, ref, a_send.at[m, s], a_recv.at[m, s], a_target[m])

    def recv_b(m, s):
        ref = block(m, b_from(m, s, core), middle)
        return remote(ref, ref, b_send.at[m, s], b_recv.at[m, s], b_target[m])

    def send_x(m, s):
        ref = block(m, a_from(m, s, core), side)
        return remote(ref, ref, x_send.at[m, s], x_recv.at[m, s], (partner, me))

    def recv_x(m, s):
        ref = block(m, a_from(m, s, core), other_side)
        return remote(ref, ref, x_send.at[m, s], x_recv.at[m, s], (partner, me))

    def share(m, s, kind, which):
        columns, origin, send, recv = {
            "a": (side, a_from, sa_send, sa_recv),
            "b": (middle, b_from, sb_send, sb_recv),
            "x": (other_side, a_from, sx_send, sx_recv),
        }[kind]
        ref = block(m, origin(m, s, which), columns)
        return remote(ref, ref, send.at[m, s], recv.at[m, s], (group, sibling))

    def first_a(m):
        return remote(
            sources[m].at[:, side], block(m, me, side), a_send.at[m, 1], a_recv.at[m, 1], a_target[m]
        )

    def first_b(m):
        return remote(
            sources[m].at[:, middle], block(m, me, middle), b_send.at[m, 1], b_recv.at[m, 1], b_target[m]
        )

    def share_own(m, e):
        return remote(sources[m], weights.at[m, e], so_send.at[m], so_recv.at[m], (group, sibling))

    def send_queries(slot, target):
        return remote(query_rows, got_queries.at[slot], q_send.at[slot], q_recv.at[slot], (group, target))

    pl.semaphore_wait(barrier, len(friends))
    for m in range(2):
        first_a(m).start()
        first_b(m).start()
    for m in range(2):
        share_own(m, me).start()

    all_queries = queries[...].astype(jnp.float32)
    for h in range(Q_HEADS):
        query_rows[pl.ds(h * STEPS, STEPS), :] = all_queries[:, h * HEAD_DIM : (h + 1) * HEAD_DIM]
    send_queries(0, left).start()
    send_queries(1, right).start()

    gains = gain[...].astype(jnp.float32)
    tile = 16

    for p in range(passages):
        loads[p].wait()

        @pl.loop(0, length // tile)
        def _(i):
            rows = pl.ds(pl.multiple_of(i * tile, tile), tile)
            x = raw[p, rows, :].astype(jnp.float32)
            scale = lax.rsqrt(jnp.mean(x * x, axis=-1, keepdims=True) + EPSILON)
            y = (x * scale * gains).astype(jnp.bfloat16)
            to = pl.ds(pl.multiple_of(p * length + i * tile, tile), tile)
            for e in range(devices):
                normed[e, to, :] = y[:, e * depth : (e + 1) * depth]

    def gemm(m, e0, e1, start, count, init=False):
        @pl.loop(0, count)
        def _(j):
            columns = pl.ds(pl.multiple_of(start + j * 256, 256), 256)
            part = jnp.dot(normed[e0], weights[m, e0, :, columns], preferred_element_type=jnp.float32)
            part += jnp.dot(normed[e1], weights[m, e1, :, columns], preferred_element_type=jnp.float32)
            if init:
                sums[m, :, columns] = part
            else:
                sums[m, :, columns] += part

    def ring(m, s):
        recv_a(m, s).wait_recv()

        @pl.when(s < chips - 1)
        def _():
            send_a(m, s + 1).start()

        send_x(m, s).start()
        share(m, s, "a", core).start()
        recv_b(m, s).wait_recv()

        @pl.when(s < chips - 1)
        def _():
            send_b(m, s + 1).start()

        share(m, s, "b", core).start()

    def cross(m, s):
        recv_x(m, s).wait_recv()
        share(m, s, "x", core).start()

    def compute_ab(m, s):
        share(m, s, "a", 1 - core).wait_recv()
        share(m, s, "b", 1 - core).wait_recv()
        gemm(m, a_from(m, s, 0), a_from(m, s, 1), odd * (SIDE + MIDDLE), SIDE // 256)
        gemm(m, b_from(m, s, 0), b_from(m, s, 1), SIDE, MIDDLE // 256)

    def compute_x(m, s):
        share(m, s, "x", 1 - core).wait_recv()
        gemm(m, a_from(m, s, 0), a_from(m, s, 1), (1 - odd) * (SIDE + MIDDLE), SIDE // 256)

    last = chips - 1
    ring(0, 1)
    for m in range(2):
        own_loads[m].wait()
        share_own(m, sibling).wait_recv()
        gemm(m, chip * 2, chip * 2 + 1, 0, (2 * SIDE + MIDDLE) // 256, init=True)

    def step(i):
        ring(0, i)
        ring(1, i - 1)
        cross(0, i - 1)
        compute_ab(0, i - 1)

        @pl.when(i >= 3)
        def _():
            cross(1, i - 2)
            compute_ab(1, i - 2)
            compute_x(0, i - 2)

        @pl.when(i >= 4)
        def _():
            compute_x(1, i - 3)

    pl.loop(2, chips)(step)

    ring(1, last)
    cross(0, last)
    cross(1, last - 1)
    compute_ab(0, last)
    compute_x(0, last - 1)
    cross(1, last)
    compute_x(0, last)

    for slot, source in ((0, right), (1, left)):
        send_queries(slot, source).wait_recv()
    for p in range(passages):
        owned_by = owner[me * passages + p]
        from_self = jnp.where(owned_by == me, 1.0, 0.0)
        from_right = jnp.where(owned_by == right, 1.0, 0.0)
        from_left = jnp.where(owned_by == left, 1.0, 0.0)
        chosen = query_rows[...] * from_self + got_queries[0] * from_right + got_queries[1] * from_left
        chosen = chosen.astype(jnp.bfloat16)
        rows = pl.ds(p * length, length)
        for g in range(KV_HEADS):
            k = sums[0, rows, g * HEAD_DIM : (g + 1) * HEAD_DIM]
            turned = k * cosines[...] + pltpu.roll(k, HEAD_DIM // 2, 1) * sines[...]
            scores[p, g * 8 : (g + 1) * 8, :] = dot_t(
                chosen[g * 8 : (g + 1) * 8, :], turned.astype(jnp.bfloat16)
            )
        w = softcap_exp(scores[p])
        dens[p] = jnp.broadcast_to(jnp.sum(w, axis=-1, keepdims=True), (ROWS, HEAD_DIM))
        scores[p] = w

    all_keys = new_keys[...].astype(jnp.float32)
    all_values = new_values[...].astype(jnp.float32)
    for g in range(KV_HEADS):
        fresh_rows[0, pl.ds(g * STEPS, STEPS), :] = all_keys[:, g * HEAD_DIM : (g + 1) * HEAD_DIM]
        fresh_rows[1, pl.ds(g * STEPS, STEPS), :] = all_values[:, g * HEAD_DIM : (g + 1) * HEAD_DIM]
    fresh = dot_t(query_rows[...].astype(jnp.bfloat16), fresh_rows[0].astype(jnp.bfloat16))
    row = lax.broadcasted_iota(jnp.int32, fresh.shape, 0)
    column = lax.broadcasted_iota(jnp.int32, fresh.shape, 1)
    seen = (row // 8 == column // STEPS) & (column % STEPS <= row % STEPS)
    fresh = jnp.where(seen, softcap_exp(fresh), 0.0)
    fresh_den = jnp.broadcast_to(jnp.sum(fresh, axis=-1, keepdims=True), (ROWS, HEAD_DIM))
    fresh_num = jnp.dot(
        fresh.astype(jnp.bfloat16), fresh_rows[1].astype(jnp.bfloat16), preferred_element_type=jnp.float32
    )

    compute_ab(1, last - 1)
    compute_x(1, last - 2)
    compute_x(1, last - 1)
    compute_ab(1, last)
    compute_x(1, last)

    for p in range(passages):
        rows = pl.ds(p * length, length)
        w = scores[p].astype(jnp.bfloat16)
        for g in range(KV_HEADS):
            v = sums[1, rows, g * HEAD_DIM : (g + 1) * HEAD_DIM].astype(jnp.bfloat16)
            nums[p, g * 8 : (g + 1) * 8, :] = jnp.dot(
                w[g * 8 : (g + 1) * 8, :], v, preferred_element_type=jnp.float32
            )

    def picked(target):
        num = jnp.zeros((ROWS, HEAD_DIM), jnp.float32)
        den = num
        for p in range(passages):
            flag = jnp.where(owner[me * passages + p] == target, 1.0, 0.0)
            num += nums[p] * flag
            den += dens[p] * flag
        return num, den

    replies = []
    for slot, target in ((0, left), (1, right)):
        num, den = picked(target)
        sent[slot, 0] = num
        sent[slot, 1] = den
        reply = remote(sent.at[slot], got.at[slot], r_send.at[slot], r_recv.at[slot], (group, target))
        reply.start()
        replies.append(reply)
    num, den = picked(me)
    num, den = num + fresh_num, den + fresh_den
    for slot in range(2):
        replies[slot].wait_recv()
        num, den = num + got[slot, 0], den + got[slot, 1]
    result = num / den
    for h in range(Q_HEADS):
        out32[:, h * HEAD_DIM : (h + 1) * HEAD_DIM] = result[h * STEPS : (h + 1) * STEPS, :]
    out[...] = out32[...].astype(jnp.bfloat16)

    for reply in replies:
        reply.wait_send()
    for slot, target in ((0, left), (1, right)):
        send_queries(slot, target).wait_send()
    for m in range(2):
        share_own(m, me).wait_send()
        first_a(m).wait_send()
        first_b(m).wait_send()

    @pl.loop(1, chips)
    def _(s):
        for m in range(2):
            send_x(m, s).wait_send()
            for kind in "abx":
                share(m, s, kind, core).wait_send()

    @pl.loop(2, chips)
    def _(s):
        for m in range(2):
            send_a(m, s).wait_send()
            send_b(m, s).wait_send()


def shards(snake, hidden, norm_gain, w_key, w_value, queries, new_keys, new_values, passage_owner):
    passages, length, width = hidden.shape
    depth, columns = w_key.shape
    devices = lax.axis_size("dev")
    chips = devices // 2
    tokens = passages * length
    cosines, sines = rotation_tables(length)
    vmem = pl.BlockSpec(memory_space=pltpu.VMEM)
    hbm = pl.BlockSpec(memory_space=pl.ANY)
    pair = pltpu.SemaphoreType.DMA((2,))
    staged = pltpu.SemaphoreType.DMA((2, chips))
    f32 = jnp.float32
    out = pl.pallas_call(
        functools.partial(kernel, snake),
        out_shape=jax.ShapeDtypeStruct((STEPS, Q_HEADS * HEAD_DIM), jnp.bfloat16),
        in_specs=[hbm, vmem, hbm, hbm, vmem, vmem, vmem, vmem, vmem, pl.BlockSpec(memory_space=pltpu.SMEM)],
        out_specs=vmem,
        scratch_shapes=[
            pltpu.VMEM((passages, length, width), jnp.bfloat16),
            pltpu.VMEM((devices, tokens, depth), jnp.bfloat16),
            pltpu.VMEM((2, devices, depth, columns), jnp.bfloat16),
            pltpu.VMEM((2, tokens, columns), f32),
            pltpu.VMEM((ROWS, HEAD_DIM), f32),
            pltpu.VMEM((2, ROWS, HEAD_DIM), f32),
            pltpu.VMEM((2, STEPS * KV_HEADS, HEAD_DIM), f32),
            pltpu.VMEM((passages, ROWS, length), f32),
            pltpu.VMEM((passages, ROWS, HEAD_DIM), f32),
            pltpu.VMEM((passages, ROWS, HEAD_DIM), f32),
            pltpu.VMEM((2, 2, ROWS, HEAD_DIM), f32),
            pltpu.VMEM((2, 2, ROWS, HEAD_DIM), f32),
            pltpu.VMEM((STEPS, Q_HEADS * HEAD_DIM), f32),
            pltpu.SemaphoreType.DMA((passages,)),
            pair,
            *[staged] * 6,
            pair,
            pair,
            *[staged] * 6,
            *[pair] * 4,
        ],
        compiler_params=pltpu.CompilerParams(
            collective_id=0, has_side_effects=True, vmem_limit_bytes=58 * 2**20
        ),
        cost_estimate=pl.CostEstimate(
            flops=4 * tokens * width * columns, bytes_accessed=2 * tokens * width, transcendentals=0
        ),
    )(
        hidden,
        norm_gain.reshape(1, width),
        w_key,
        w_value,
        queries[0],
        new_keys[0],
        new_values[0],
        cosines,
        sines,
        passage_owner,
    )
    return out[None]


def solution(mesh):
    snake = mesh.shape["groups"] == 2
    return jax.shard_map(
        functools.partial(shards, snake),
        mesh=mesh,
        in_specs=(
            P(("groups", "dev"), None, None),
            P(),
            P("dev", None),
            P("dev", None),
            P(("groups", "dev"), None, None),
            P(("groups", "dev"), None, None),
            P(("groups", "dev"), None, None),
            P("groups"),
        ),
        out_specs=P(("groups", "dev"), None, None),
        check_vma=False,
    )
```

```python
import functools

import jax
import jax.numpy as jnp
import numpy as np
from jax import lax
from jax.experimental import pallas as pl
from jax.experimental.pallas import tpu as pltpu
from jax.sharding import PartitionSpec as P

HEAD_DIM = 128
KV_HEADS = 8
Q_HEADS = 16
STEPS = 4
ROWS = STEPS * Q_HEADS

CAP_LIMIT = 50.0
QUERY_SCALE = 1.0 / 12.0
EPSILON = 1e-06

SIDE = (256, 384)
MIDDLE = (512, 256)
SHIFT = (768, 640)
STREAMS = (
    (0, 0, 128, 256, 256),
    (0, 128, 128, 512, 256),
    (1, 0, 128, 384, 128),
    (1, 128, 256, 512, 128),
)
MESH = pl.DeviceIdType.MESH


def rotation_tables(length):
    half = HEAD_DIM // 2
    inverse = 10000.0 ** (-(np.arange(half, dtype=np.float64) * 2.0) / HEAD_DIM)
    angles = np.arange(length, dtype=np.float64)[:, None] * inverse[None, :]
    cosine, sine = np.cos(angles), np.sin(angles)
    return (
        np.concatenate([cosine, cosine], axis=1).astype(np.float32),
        np.concatenate([-sine, sine], axis=1).astype(np.float32),
    )


def softcap_exp(scores):
    return jnp.exp(CAP_LIMIT * jnp.tanh(scores * (QUERY_SCALE / CAP_LIMIT)))


def dot_t(a, b):
    return lax.dot_general(a, b, (((1,), (1,)), ((), ())), preferred_element_type=jnp.float32)


def kernel(
    snake, hidden, gain, w_key, w_value, queries, new_keys, new_values, cosines, sines, owner,
    out,
    raw, normed, weights, sums, query_rows, got_queries, fresh_rows, scores, dens, nums, sent, got, out32,
    hidden_sem, own_sem, a_send, a_recv, b_send, b_recv, x_send, x_recv,
    so_send, so_recv, sa_send, sa_recv, sb_send, sb_recv, sx_send, sx_recv,
    q_send, q_recv, r_send, r_recv,
):
    devices = lax.axis_size("dev")
    chips = devices // 2
    group = lax.axis_index("groups")
    me = lax.axis_index("dev")
    chip, core = me // 2, me % 2
    odd = group % 2
    partner = group + 1 - 2 * odd
    passages, length, width = hidden.shape
    depth = width // devices

    def chip_at(place):
        place = lax.rem(place + 2 * chips, chips)
        if not snake:
            return place
        return jnp.where(place < chips // 2, 2 * place, 2 * (chips - 1 - place) + 1)

    if snake:
        place = jnp.where(chip % 2 == 0, chip // 2, chips - 1 - chip // 2)
    else:
        place = chip

    def device_at(position, which):
        return chip_at(position) * 2 + which

    ahead, behind = device_at(place + 1, core), device_at(place - 1, core)
    sibling = chip * 2 + 1 - core
    right, left = lax.rem(me + 1, devices), lax.rem(me + devices - 1, devices)

    barrier = pltpu.get_barrier_semaphore()
    friends = [(group, ahead), (group, behind), (group, sibling), (partner, me), (group, right), (group, left)]
    for friend in friends:
        pl.semaphore_signal(barrier, inc=1, device_id=friend, device_id_type=MESH)

    loads = [
        pltpu.make_async_copy(hidden.at[p], raw.at[p], hidden_sem.at[p]) for p in range(passages)
    ]
    for load in loads:
        load.start()
    sources = (w_key, w_value)
    own_loads = [
        pltpu.make_async_copy(sources[m], weights.at[m, me], own_sem.at[m]) for m in range(2)
    ]
    for load in own_loads:
        load.start()

    def side(k):
        m, start, size, _, _ = STREAMS[k]
        return pl.ds(pl.multiple_of(start + odd * SHIFT[m], 128), size)

    def other_side(k):
        m, start, size, _, _ = STREAMS[k]
        return pl.ds(pl.multiple_of(start + (1 - odd) * SHIFT[m], 128), size)

    def middle(k):
        return pl.ds(STREAMS[k][3], STREAMS[k][4])

    def remote(src, dst, send, recv, target):
        return pltpu.make_async_remote_copy(
            src_ref=src, dst_ref=dst, send_sem=send, recv_sem=recv, device_id=target, device_id_type=MESH
        )

    a_target = (group, jnp.where(core == 0, ahead, behind))
    b_target = (group, jnp.where(core == 0, behind, ahead))

    def block(k, e, columns):
        return weights.at[STREAMS[k][0], e, :, columns]

    def a_from(s, which):
        return device_at(place - (1 - 2 * which) * s, which)

    def b_from(s, which):
        return device_at(place + (1 - 2 * which) * s, which)

    def send_a(k, s):
        ref = block(k, a_from(s - 1, core), side(k))
        return remote(ref, ref, a_send.at[k, s], a_recv.at[k, s], a_target)

    def send_b(k, s):
        ref = block(k, b_from(s - 1, core), middle(k))
        return remote(ref, ref, b_send.at[k, s], b_recv.at[k, s], b_target)

    def recv_a(k, s):
        ref = block(k, a_from(s, core), side(k))
        return remote(ref, ref, a_send.at[k, s], a_recv.at[k, s], a_target)

    def recv_b(k, s):
        ref = block(k, b_from(s, core), middle(k))
        return remote(ref, ref, b_send.at[k, s], b_recv.at[k, s], b_target)

    def send_x(k, s):
        ref = block(k, a_from(s, core), side(k))
        return remote(ref, ref, x_send.at[k, s], x_recv.at[k, s], (partner, me))

    def recv_x(k, s):
        ref = block(k, a_from(s, core), other_side(k))
        return remote(ref, ref, x_send.at[k, s], x_recv.at[k, s], (partner, me))

    def share(k, s, kind, which):
        columns, origin, send, recv = {
            "a": (side, a_from, sa_send, sa_recv),
            "b": (middle, b_from, sb_send, sb_recv),
            "x": (other_side, a_from, sx_send, sx_recv),
        }[kind]
        ref = block(k, origin(s, which), columns(k))
        return remote(ref, ref, send.at[k, s], recv.at[k, s], (group, sibling))

    def first_a(k):
        source = sources[STREAMS[k][0]].at[:, side(k)]
        return remote(source, block(k, me, side(k)), a_send.at[k, 1], a_recv.at[k, 1], a_target)

    def first_b(k):
        source = sources[STREAMS[k][0]].at[:, middle(k)]
        return remote(source, block(k, me, middle(k)), b_send.at[k, 1], b_recv.at[k, 1], b_target)

    def share_own(m, e):
        return remote(sources[m], weights.at[m, e], so_send.at[m], so_recv.at[m], (group, sibling))

    def send_queries(slot, target):
        return remote(query_rows, got_queries.at[slot], q_send.at[slot], q_recv.at[slot], (group, target))

    pl.semaphore_wait(barrier, len(friends))
    def first(m):
        for k in (2 * m, 2 * m + 1):
            first_a(k).start()
            first_b(k).start()
        share_own(m, me).start()

    first(0)

    all_queries = queries[...].astype(jnp.float32)
    for h in range(Q_HEADS):
        query_rows[pl.ds(h * STEPS, STEPS), :] = all_queries[:, h * HEAD_DIM : (h + 1) * HEAD_DIM]
    send_queries(0, left).start()
    send_queries(1, right).start()

    gains = gain[...].astype(jnp.float32)[None, :]
    tile = 16

    def normalize(p, begin, end):
        @pl.loop(begin // tile, end // tile)
        def _(i):
            rows = pl.ds(pl.multiple_of(i * tile, tile), tile)
            x = raw[p, rows, :].astype(jnp.float32)
            scale = lax.rsqrt(jnp.mean(x * x, axis=-1, keepdims=True) + EPSILON)
            y = (x * scale * gains).astype(jnp.bfloat16)
            to = pl.ds(pl.multiple_of(p * length + i * tile, tile), tile)
            for e in range(devices):
                normed[e, to, :] = y[:, e * depth : (e + 1) * depth]

    def gemm(m, e0, e1, start, width, init=False):
        size = width if width < 512 else 256

        @pl.loop(0, width // size)
        def _(j):
            columns = pl.ds(pl.multiple_of(start + j * size, 128), size)
            part = jnp.dot(normed[e0], weights[m, e0, :, columns], preferred_element_type=jnp.float32)
            part += jnp.dot(normed[e1], weights[m, e1, :, columns], preferred_element_type=jnp.float32)
            if init:
                sums[m, :, columns] = part
            else:
                sums[m, :, columns] += part

    def ring(k, s):
        recv_a(k, s).wait_recv()

        @pl.when(s < chips - 1)
        def _():
            send_a(k, s + 1).start()

        send_x(k, s).start()
        share(k, s, "a", core).start()
        recv_b(k, s).wait_recv()

        @pl.when(s < chips - 1)
        def _():
            send_b(k, s + 1).start()

        share(k, s, "b", core).start()

    def cross(m, s):
        for k in (2 * m, 2 * m + 1):
            recv_x(k, s).wait_recv()
            share(k, s, "x", core).start()

    def compute(m, s, kind):
        for k in (2 * m, 2 * m + 1):
            share(k, s, kind, 1 - core).wait_recv()
        if kind == "b":
            gemm(m, b_from(s, 0), b_from(s, 1), SIDE[m], MIDDLE[m])
        else:
            start = (odd if kind == "a" else 1 - odd) * SHIFT[m]
            gemm(m, a_from(s, 0), a_from(s, 1), start, SIDE[m])

    last = chips - 1
    split = length // 2 // tile * tile
    loads[0].wait()
    normalize(0, 0, split)
    first(1)
    normalize(0, split, length)
    for p in range(1, passages):
        loads[p].wait()
        if p == 1:
            ring(0, 1)
        normalize(p, 0, split)
        if p == 1:
            ring(1, 1)
        normalize(p, split, length)
    for m in range(2):
        own_loads[m].wait()
        share_own(m, sibling).wait_recv()
        gemm(m, chip * 2, chip * 2 + 1, 0, 2 * SIDE[m] + MIDDLE[m], init=True)

    def step(i):
        ring(0, i)
        compute(0, i - 1, "b")
        ring(2, i - 1)
        cross(0, i - 1)

        @pl.when(i >= 3)
        def _():
            compute(1, i - 2, "a")

        ring(1, i)
        compute(0, i - 1, "a")

        @pl.when(i >= 3)
        def _():
            compute(0, i - 2, "x")

        ring(3, i - 1)

        @pl.when(i >= 3)
        def _():
            cross(1, i - 2)
            compute(1, i - 2, "b")

        @pl.when(i >= 4)
        def _():
            compute(1, i - 3, "x")

    pl.loop(2, chips)(step)

    ring(2, last)
    cross(0, last)
    compute(0, last, "b")
    ring(3, last)
    cross(1, last - 1)
    compute(0, last, "a")
    compute(0, last - 1, "x")
    compute(0, last, "x")

    for slot, source in ((0, right), (1, left)):
        send_queries(slot, source).wait_recv()
    for p in range(passages):
        if p == 1:
            cross(1, last)
        owned_by = owner[me * passages + p]
        from_self = jnp.where(owned_by == me, 1.0, 0.0)
        from_right = jnp.where(owned_by == right, 1.0, 0.0)
        from_left = jnp.where(owned_by == left, 1.0, 0.0)
        chosen = query_rows[...] * from_self + got_queries[0] * from_right + got_queries[1] * from_left
        chosen = chosen.astype(jnp.bfloat16)
        rows = pl.ds(p * length, length)
        for g in range(KV_HEADS):
            k = sums[0, rows, g * HEAD_DIM : (g + 1) * HEAD_DIM]
            turned = k * cosines[...] + pltpu.roll(k, HEAD_DIM // 2, 1) * sines[...]
            scores[p, g * 8 : (g + 1) * 8, :] = dot_t(
                chosen[g * 8 : (g + 1) * 8, :], turned.astype(jnp.bfloat16)
            )
        w = softcap_exp(scores[p])
        dens[p] = jnp.broadcast_to(jnp.sum(w, axis=-1, keepdims=True), (ROWS, HEAD_DIM))
        scores[p] = w

    all_keys = new_keys[...].astype(jnp.float32)
    all_values = new_values[...].astype(jnp.float32)
    for g in range(KV_HEADS):
        fresh_rows[0, pl.ds(g * STEPS, STEPS), :] = all_keys[:, g * HEAD_DIM : (g + 1) * HEAD_DIM]
        fresh_rows[1, pl.ds(g * STEPS, STEPS), :] = all_values[:, g * HEAD_DIM : (g + 1) * HEAD_DIM]
    fresh = dot_t(query_rows[...].astype(jnp.bfloat16), fresh_rows[0].astype(jnp.bfloat16))
    row = lax.broadcasted_iota(jnp.int32, fresh.shape, 0)
    column = lax.broadcasted_iota(jnp.int32, fresh.shape, 1)
    seen = (row // 8 == column // STEPS) & (column % STEPS <= row % STEPS)
    fresh = jnp.where(seen, softcap_exp(fresh), 0.0)
    fresh_den = jnp.broadcast_to(jnp.sum(fresh, axis=-1, keepdims=True), (ROWS, HEAD_DIM))
    fresh_num = jnp.dot(
        fresh.astype(jnp.bfloat16), fresh_rows[1].astype(jnp.bfloat16), preferred_element_type=jnp.float32
    )

    compute(1, last - 1, "a")
    compute(1, last - 1, "b")
    compute(1, last - 2, "x")
    compute(1, last - 1, "x")
    compute(1, last, "a")
    compute(1, last, "b")
    compute(1, last, "x")

    for p in range(passages):
        rows = pl.ds(p * length, length)
        w = scores[p].astype(jnp.bfloat16)
        for g in range(KV_HEADS):
            v = sums[1, rows, g * HEAD_DIM : (g + 1) * HEAD_DIM].astype(jnp.bfloat16)
            nums[p, g * 8 : (g + 1) * 8, :] = jnp.dot(
                w[g * 8 : (g + 1) * 8, :], v, preferred_element_type=jnp.float32
            )

    def picked(target):
        num = jnp.zeros((ROWS, HEAD_DIM), jnp.float32)
        den = num
        for p in range(passages):
            flag = jnp.where(owner[me * passages + p] == target, 1.0, 0.0)
            num += nums[p] * flag
            den += dens[p] * flag
        return num, den

    replies = []
    for slot, target in ((0, left), (1, right)):
        num, den = picked(target)
        sent[slot, 0] = num
        sent[slot, 1] = den
        reply = remote(sent.at[slot], got.at[slot], r_send.at[slot], r_recv.at[slot], (group, target))
        reply.start()
        replies.append(reply)
    num, den = picked(me)
    num, den = num + fresh_num, den + fresh_den
    for slot in range(2):
        replies[slot].wait_recv()
        num, den = num + got[slot, 0], den + got[slot, 1]
    result = num / den
    for h in range(Q_HEADS):
        out32[:, h * HEAD_DIM : (h + 1) * HEAD_DIM] = result[h * STEPS : (h + 1) * STEPS, :]
    out[...] = out32[...].astype(jnp.bfloat16)

    for reply in replies:
        reply.wait_send()
    for slot, target in ((0, left), (1, right)):
        send_queries(slot, target).wait_send()
    for m in range(2):
        share_own(m, me).wait_send()
    for k in range(len(STREAMS)):
        first_a(k).wait_send()
        first_b(k).wait_send()

    @pl.loop(1, chips)
    def _(s):
        for k in range(len(STREAMS)):
            send_x(k, s).wait_send()
            for kind in "abx":
                share(k, s, kind, core).wait_send()

    @pl.loop(2, chips)
    def _(s):
        for k in range(len(STREAMS)):
            send_a(k, s).wait_send()
            send_b(k, s).wait_send()


def shards(snake, hidden, norm_gain, w_key, w_value, queries, new_keys, new_values, passage_owner):
    passages, length, width = hidden.shape
    depth, columns = w_key.shape
    devices = lax.axis_size("dev")
    chips = devices // 2
    tokens = passages * length
    cosines, sines = rotation_tables(length)
    vmem = pl.BlockSpec(memory_space=pltpu.VMEM)
    hbm = pl.BlockSpec(memory_space=pl.ANY)
    pair = pltpu.SemaphoreType.DMA((2,))
    staged = pltpu.SemaphoreType.DMA((len(STREAMS), chips))
    f32 = jnp.float32
    out = pl.pallas_call(
        functools.partial(kernel, snake),
        out_shape=jax.ShapeDtypeStruct((STEPS, Q_HEADS * HEAD_DIM), jnp.bfloat16),
        in_specs=[hbm, vmem, hbm, hbm, vmem, vmem, vmem, vmem, vmem, pl.BlockSpec(memory_space=pltpu.SMEM)],
        out_specs=vmem,
        scratch_shapes=[
            pltpu.VMEM((passages, length, width), jnp.bfloat16),
            pltpu.VMEM((devices, tokens, depth), jnp.bfloat16),
            pltpu.VMEM((2, devices, depth, columns), jnp.bfloat16),
            pltpu.VMEM((2, tokens, columns), f32),
            pltpu.VMEM((ROWS, HEAD_DIM), f32),
            pltpu.VMEM((2, ROWS, HEAD_DIM), f32),
            pltpu.VMEM((2, STEPS * KV_HEADS, HEAD_DIM), f32),
            pltpu.VMEM((passages, ROWS, length), f32),
            pltpu.VMEM((passages, ROWS, HEAD_DIM), f32),
            pltpu.VMEM((passages, ROWS, HEAD_DIM), f32),
            pltpu.VMEM((2, 2, ROWS, HEAD_DIM), f32),
            pltpu.VMEM((2, 2, ROWS, HEAD_DIM), f32),
            pltpu.VMEM((STEPS, Q_HEADS * HEAD_DIM), f32),
            pltpu.SemaphoreType.DMA((passages,)),
            pair,
            *[staged] * 6,
            pair,
            pair,
            *[staged] * 6,
            *[pair] * 4,
        ],
        compiler_params=pltpu.CompilerParams(
            collective_id=0, has_side_effects=True, vmem_limit_bytes=58 * 2**20
        ),
        cost_estimate=pl.CostEstimate(
            flops=4 * tokens * width * columns, bytes_accessed=2 * tokens * width, transcendentals=0
        ),
    )(
        hidden,
        norm_gain,
        w_key,
        w_value,
        queries[0],
        new_keys[0],
        new_values[0],
        cosines,
        sines,
        passage_owner,
    )
    return out[None]


def solution(mesh):
    snake = mesh.shape["groups"] == 2
    return jax.shard_map(
        functools.partial(shards, snake),
        mesh=mesh,
        in_specs=(
            P(("groups", "dev"), None, None),
            P(),
            P("dev", None),
            P("dev", None),
            P(("groups", "dev"), None, None),
            P(("groups", "dev"), None, None),
            P(("groups", "dev"), None, None),
            P("groups"),
        ),
        out_specs=P(("groups", "dev"), None, None),
        check_vma=False,
    )
```
